32 devices in a mesh: groups: 2 (over x), loop: 16 (over z, y, core).
Axes of the slice: x: 2, y: 2, z: 4, core: 2. Of those that a mesh axis runs over, the one named last changes fastest.
Arguments:
- tokens: bfloat16 [2048, 4096], P(('groups', 'loop')), parts along dimension 0, may hold values from -6 to 6
- expert_ids: int32 [2048, 8], P(('groups', 'loop')), parts along dimension 0, may hold values from 0 to 127, as said below
- keep_mask: int32 [2048, 8], P(('groups', 'loop')), parts along dimension 0, may hold values from 0 to 1, as said below
- tile_slot: int32 [2048, 8], P(('groups', 'loop')), parts along dimension 0, may hold values from 0 to 95, as said below
- route_weight: float32 [2048, 8], P(('groups', 'loop')), parts along dimension 0, may hold values from 0.2 to 1
- gate_weight: bfloat16 [16, 4096, 384], P('loop'), may hold values from -0.09375 to 0.09375
- up_weight: bfloat16 [16, 4096, 384], P('loop'), may hold values from -0.09375 to 0.09375
- down_weight: bfloat16 [16, 384, 4096], P('loop'), may hold values from -0.15625 to 0.15625
Outputs:
- mixed: bfloat16 [2048, 4096], P(('groups', 'loop')), parts along dimension 0
The draws below stay inside these ranges and needn't reach their ends.
There are 2 independent parts, one for each index of `groups`. The reference program is written for one: setup_inputs(seed, part) draws one part's arguments, and reference() takes and returns one part's arrays. A program takes and returns all parts, laid end to end along the dimension named above; an argument that names none is the same for every part. Nothing has to cross between parts.
Inputs may be any that keep to these rules, and one draw needn't show every extreme that they name: `expert_ids`: each row names 8 different experts. `keep_mask`: of one device's rows at most 8 kept entries name one expert, and the kept entries of one expert fit its 96 slots. `tile_slot`: where keep_mask is 1, the entries naming one expert have distinct slots; in every draw some expert below 4 gets 8 kept entries from the rows of several devices and fills all 96 slots.
All inputs are finite; a program needn't handle non-finite values.
Results may differ from the reference program's by a relative error of at most 0.0059.
Values may be sent and summed in bfloat16 or wider, within the bound.
A program may use at most 64 MiB of HBM per device.

```python
import jax
import jax.numpy as jnp
from jax import lax

D = 4096
FF = 1536
EXPERTS = 128
TOP = 8
SLICES = 4
ROWS_DEV = 64
SEND = 8
EXP_GROUP = 4
HS = 384
CAP = 96
TOKENS = 1024


def routing_tables(key):
    key_level, key_hot, key_noise, key_order = jax.random.split(key, 4)
    devices_loop = TOKENS // ROWS_DEV
    level = jax.random.randint(key_level, (EXPERTS,), 0, 3) * 256
    hot_expert = jax.random.randint(key_hot, (), 0, EXP_GROUP)
    bias = jnp.where(jnp.arange(EXPERTS) == hot_expert, 8192, level)
    noise = jax.random.randint(key_noise, (TOKENS, EXPERTS), 0, 4096)
    score = (noise + bias[None, :]) * EXPERTS + jnp.arange(EXPERTS)[None, :]
    _, chosen = lax.top_k(score, TOP)
    chosen = chosen.astype(jnp.int32)
    one_hot = (chosen[:, :, None] == jnp.arange(EXPERTS)[None, None, :]).astype(jnp.int32)
    per_device = one_hot.reshape(devices_loop, ROWS_DEV * TOP, EXPERTS)
    order = jax.random.permutation(key_order, ROWS_DEV * TOP)
    shuffled = per_device[:, order, :]
    earlier = jnp.cumsum(shuffled, axis=1) - shuffled
    rank_shuffled = jnp.sum(earlier * shuffled, axis=2)
    local_rank = jnp.zeros((devices_loop, ROWS_DEV * TOP), jnp.int32).at[:, order].set(rank_shuffled.astype(jnp.int32))
    local_keep = (local_rank < SEND).astype(jnp.int32)
    counts = jnp.sum(per_device * local_keep[:, :, None], axis=1)
    offsets = jnp.cumsum(counts, axis=0) - counts
    global_slot = jnp.sum(per_device * offsets[:, None, :], axis=2) + local_rank
    kept = local_keep * (global_slot < CAP).astype(jnp.int32)
    slots = jnp.minimum(global_slot, CAP - 1)
    return (chosen, kept.reshape(TOKENS, TOP).astype(jnp.int32), slots.reshape(TOKENS, TOP).astype(jnp.int32))


def draw_expert_ids(key, part):
    tables = routing_tables(key)
    return tables[0]


def draw_keep_mask(key, part):
    tables = routing_tables(key)
    return tables[1]


def draw_tile_slot(key, part):
    tables = routing_tables(key)
    return tables[2]


def block_levels(stream_key, extent, cuts, least, top_value):
    def one(dim, parts):
        heights = jax.random.uniform(jax.random.fold_in(jax.random.fold_in(stream_key, 6), dim), (parts,), jnp.float32, least / len(cuts), top_value / len(cuts))
        return jnp.repeat(jnp.exp(heights), extent[dim] // parts).reshape((-1,) + (1,) * (len(extent) - dim - 1))

    loudness = one(*cuts[0])
    for cut in cuts[1:]:
        loudness = loudness * one(*cut)
    return loudness


def scatter_about(own_key, shape, spread, bound, pieces=(), kind=jnp.bfloat16):
    drawn = jax.random.normal(own_key, shape, jnp.float32) * spread
    if len(pieces) > 0:
        drawn = block_levels(own_key, shape, pieces, -0.22, 0.18) * drawn
    return jnp.clip(drawn, min=-bound, max=bound).astype(kind)


def setup_inputs(seed: int = 0, part: int = 0) -> dict:
    key_list = jax.random.split(jax.random.key(seed), 9)
    part_keys = jax.random.split(jax.random.fold_in(key_list[8], part), 9)
    return {
        "tokens": scatter_about(part_keys[0], (TOKENS, D), 1.0, 6.0, ((0, 16),)),
        "expert_ids": draw_expert_ids(jax.random.fold_in(jax.random.fold_in(key_list[8], part), 71), part),
        "keep_mask": draw_keep_mask(jax.random.fold_in(jax.random.fold_in(key_list[8], part), 71), part),
        "tile_slot": draw_tile_slot(jax.random.fold_in(jax.random.fold_in(key_list[8], part), 71), part),
        "route_weight": jnp.clip(0.2 + 0.8 * jax.random.uniform(part_keys[4], (TOKENS, TOP), jnp.float32) ** block_levels(part_keys[4], (TOKENS, TOP), ((0, 16),), -0.2, 0.2), 0.2, 1.0),
        "gate_weight": scatter_about(key_list[5], (EXP_GROUP * SLICES, D, HS), D ** -0.5, 0.09375, ((0, 16),)),
        "up_weight": scatter_about(key_list[6], (EXP_GROUP * SLICES, D, HS), D ** -0.5, 0.09375, ((0, 16),)),
        "down_weight": scatter_about(key_list[7], (EXP_GROUP * SLICES, HS, D), FF ** -0.5, 0.15625, ((0, 16),)),
    }


def reference(tokens, expert_ids, keep_mask, tile_slot, route_weight, gate_weight, up_weight, down_weight):
    live_entry = (expert_ids < EXP_GROUP) & (keep_mask == 1)

    def one_expert(total, expert):
        match = live_entry & (expert_ids == expert)
        has_entry = jnp.any(match, axis=1)
        slot_row = jnp.sum(jnp.where(match, tile_slot, 0), axis=1).astype(jnp.int32)
        index = jnp.where(has_entry, slot_row, CAP).astype(jnp.int32)
        expert_tile = jnp.zeros((CAP, D), jnp.bfloat16).at[index].set(tokens, mode="drop")
        start = (expert * SLICES).astype(jnp.int32)
        gate_full = jnp.transpose(lax.dynamic_slice_in_dim(gate_weight, start, SLICES, 0), (1, 0, 2)).reshape(D, FF)
        up_full = jnp.transpose(lax.dynamic_slice_in_dim(up_weight, start, SLICES, 0), (1, 0, 2)).reshape(D, FF)
        down_full = lax.dynamic_slice_in_dim(down_weight, start, SLICES, 0).reshape(FF, D)
        gate_out = jnp.dot(expert_tile, gate_full, preferred_element_type=jnp.float32)
        up_out = jnp.dot(expert_tile, up_full, preferred_element_type=jnp.float32)
        hidden = (jax.nn.silu(gate_out) * up_out).astype(jnp.bfloat16)
        expert_out = jnp.dot(hidden, down_full, preferred_element_type=jnp.float32).astype(jnp.bfloat16)
        weight_row = jnp.sum(jnp.where(match, route_weight, jnp.zeros_like(route_weight)), axis=1)
        picked = jnp.take(expert_out, jnp.minimum(slot_row, CAP - 1).astype(jnp.int32), axis=0)
        return total + weight_row[:, None] * picked.astype(jnp.float32), None

    total, _ = lax.scan(one_expert, jnp.zeros((TOKENS, D), jnp.float32), jnp.arange(EXP_GROUP, dtype=jnp.int32))
    return total.astype(jnp.bfloat16)
```

```python
import functools

import jax
import jax.numpy as jnp
from jax import lax
from jax.experimental import pallas as pl
from jax.experimental.pallas import tpu as pltpu
from jax.sharding import PartitionSpec as P

SLICES = 4
SEND = 8
CHUNKS = 4
MESH = pl.DeviceIdType.MESH


def kernel(
    experts,
    tokens, ids, keep, route, gate_hbm, up_hbm, down_hbm,
    out,
    outgoing, tile, gate_w, up_w, down_w, gate_acc, up_acc, own_part,
    core_out, core_in, side_out, side_in, back_out, back_in,
    weight_sem, z_send, z_recv, y_send, y_recv, c_send, c_recv,
    cb_send, cb_recv, yb_send, yb_recv, zb_send, zb_recv,
):
    place = lax.axis_index("loop")
    mine = lax.div(place, SLICES)
    part = lax.rem(place, SLICES)
    side = mine * SLICES + lax.rem(part + 2, SLICES)
    core = mine * SLICES + part + 1 - 2 * lax.rem(part, 2)

    def along(step):
        return lax.rem(mine + step + experts, experts) * SLICES + part

    chunks = outgoing.shape[0]
    width = outgoing.shape[-1]
    span = 2 * width
    block = 2 * SEND
    columns = experts * block
    rows = SLICES * experts * SEND

    barrier = pltpu.get_barrier_semaphore()
    for step in range(1, experts):
        pl.semaphore_signal(barrier, inc=1, device_id={"loop": along(step)}, device_id_type=MESH)
    pl.semaphore_signal(barrier, inc=1, device_id={"loop": side}, device_id_type=MESH)
    pl.semaphore_signal(barrier, inc=1, device_id={"loop": core}, device_id_type=MESH)

    loads = []
    for k in range(chunks):
        at = pl.ds(k * span, span)
        loads.append((
            pltpu.make_async_copy(gate_hbm.at[0, at], gate_w.at[at], weight_sem.at[0, k]),
            pltpu.make_async_copy(up_hbm.at[0, at], up_w.at[at], weight_sem.at[1, k]),
        ))
        for load in loads[-1]:
            load.start()
    down_load = pltpu.make_async_copy(down_hbm.at[0], down_w, weight_sem.at[2, 0])
    down_load.start()

    row_count = tokens.shape[0]
    column = lax.broadcasted_iota(jnp.int32, (row_count, columns), 1)
    expert_of = lax.rem(mine - lax.div(column, block) + experts, experts)
    position_of = lax.rem(column, SEND)
    lower = lax.rem(column, block) < SEND
    chosen = jnp.where(keep[...] == 1, ids[...], -1)
    weights = route[...]
    live = jnp.zeros((row_count, columns), jnp.float32)
    scale = jnp.zeros((row_count, columns), jnp.float32)
    for k in range(ids.shape[1]):
        match = chosen[:, k:k + 1] == expert_of
        live = jnp.where(match, 1.0, live)
        scale = jnp.where(match, weights[:, k:k + 1], scale)
    earlier = (
        lax.broadcasted_iota(jnp.int32, (row_count, row_count), 1)
        < lax.broadcasted_iota(jnp.int32, (row_count, row_count), 0)
    ).astype(jnp.bfloat16)
    before = jnp.dot(earlier, live.astype(jnp.bfloat16), preferred_element_type=jnp.float32)
    select = jnp.where(before == position_of.astype(jnp.float32), live, 0.0)
    select_low = jnp.where(lower, select, 0.0)
    select_high = jnp.where(lower, 0.0, select)
    pick = jnp.concatenate([select_low, select_high], axis=0).astype(jnp.bfloat16)

    def z_copy(k, d):
        return pltpu.make_async_remote_copy(
            src_ref=outgoing.at[k, d], dst_ref=tile.at[k, 0, d],
            send_sem=z_send.at[k], recv_sem=z_recv.at[k],
            device_id={"loop": along(-d)}, device_id_type=MESH,
        )

    def z_all(k):
        return pltpu.make_async_remote_copy(
            src_ref=outgoing.at[k, pl.ds(1, experts - 1)],
            dst_ref=tile.at[k, 0, pl.ds(1, experts - 1)],
            send_sem=z_send.at[k], recv_sem=z_recv.at[k],
            device_id={"loop": along(1)}, device_id_type=MESH,
        )

    def y_copy(k):
        return pltpu.make_async_remote_copy(
            src_ref=tile.at[k, 0], dst_ref=tile.at[k, 1],
            send_sem=y_send.at[k], recv_sem=y_recv.at[k],
            device_id={"loop": side}, device_id_type=MESH,
        )

    def c_copy(k):
        return pltpu.make_async_remote_copy(
            src_ref=tile.at[k, pl.ds(0, 2)], dst_ref=tile.at[k, pl.ds(2, 2)],
            send_sem=c_send.at[k], recv_sem=c_recv.at[k],
            device_id={"loop": core}, device_id_type=MESH,
        )

    for k in range(chunks):
        low = tokens[:, k * span:k * span + width]
        high = tokens[:, k * span + width:(k + 1) * span]
        picked = lax.dot_general(
            pick, jnp.concatenate([low, high], axis=0), (((0,), (0,)), ((), ())),
            preferred_element_type=jnp.float32,
        ).astype(jnp.bfloat16).reshape(experts, block, width)
        outgoing[k] = picked
        tile[k, 0, 0] = picked[0]
        if k == 0:
            pl.semaphore_wait(barrier, experts + 1)
        for d in range(1, experts):
            z_copy(k, d).start()

    def gate_up(k):
        arrived = tile[k].astype(jnp.float32).reshape(SLICES * experts, block, width)
        x = jnp.concatenate(
            [arrived[:, :SEND].reshape(rows, width), arrived[:, SEND:].reshape(rows, width)], axis=1
        ).astype(jnp.bfloat16)
        for load in loads[k]:
            load.wait()
        at = pl.ds(k * span, span)
        gate = jnp.dot(x, gate_w[at], preferred_element_type=jnp.float32)
        up = jnp.dot(x, up_w[at], preferred_element_type=jnp.float32)
        if k == 0:
            gate_acc[...] = gate
            up_acc[...] = up
        else:
            gate_acc[...] += gate
            up_acc[...] += up

    for t in range(chunks + 2):
        if t < chunks:
            z_all(t).wait_recv()
            y_copy(t).start()
        if 0 <= t - 1 < chunks:
            y_copy(t - 1).wait_recv()
            c_copy(t - 1).start()
        if 0 <= t - 2 < chunks:
            c_copy(t - 2).wait_recv()
            gate_up(t - 2)

    gate = gate_acc[...]
    hidden = (gate / (1.0 + jnp.exp(-gate)) * up_acc[...]).astype(jnp.bfloat16)
    down_load.wait()

    def cb_copy(k):
        return pltpu.make_async_remote_copy(
            src_ref=core_out.at[k], dst_ref=core_in.at[k],
            send_sem=cb_send.at[k], recv_sem=cb_recv.at[k],
            device_id={"loop": core}, device_id_type=MESH,
        )

    def yb_copy(k):
        return pltpu.make_async_remote_copy(
            src_ref=side_out.at[k], dst_ref=side_in.at[k],
            send_sem=yb_send.at[k], recv_sem=yb_recv.at[k],
            device_id={"loop": side}, device_id_type=MESH,
        )

    def zb_copy(k, d):
        return pltpu.make_async_remote_copy(
            src_ref=back_out.at[k, d], dst_ref=back_in.at[k, d],
            send_sem=zb_send.at[k], recv_sem=zb_recv.at[k],
            device_id={"loop": along(d)}, device_id_type=MESH,
        )

    def zb_all(k):
        return pltpu.make_async_remote_copy(
            src_ref=back_out.at[k, pl.ds(1, experts - 1)],
            dst_ref=back_in.at[k, pl.ds(1, experts - 1)],
            send_sem=zb_send.at[k], recv_sem=zb_recv.at[k],
            device_id={"loop": along(1)}, device_id_type=MESH,
        )

    scaled = jnp.concatenate([select_low * scale, select_high * scale], axis=0)
    coarse = scaled.astype(jnp.bfloat16)
    fine = (scaled - coarse.astype(jnp.float32)).astype(jnp.bfloat16)
    mixing = jnp.concatenate([coarse, fine], axis=0)

    def down(k):
        y = jnp.dot(hidden, down_w[:, k * span:(k + 1) * span], preferred_element_type=jnp.float32)
        y = jnp.concatenate(
            [
                y[:, :width].reshape(SLICES * experts, SEND, width),
                y[:, width:].reshape(SLICES * experts, SEND, width),
            ],
            axis=1,
        ).reshape(SLICES, experts, block, width)
        core_out[k] = y[2:].astype(jnp.bfloat16)
        cb_copy(k).start()
        own_part[k] = y[:2]

    def core_sum(k):
        cb_copy(k).wait_recv()
        side_out[k] = (own_part[k, 1] + core_in[k, 1].astype(jnp.float32)).astype(jnp.bfloat16)
        yb_copy(k).start()
        own_part[k, 0] = own_part[k, 0] + core_in[k, 0].astype(jnp.float32)

    def side_sum(k):
        yb_copy(k).wait_recv()
        total = (own_part[k, 0] + side_in[k].astype(jnp.float32)).astype(jnp.bfloat16)
        back_out[k] = total
        for d in range(1, experts):
            zb_copy(k, d).start()
        back_in[k, 0] = total[0]

    def mix(k):
        zb_all(k).wait_recv()
        m = jnp.dot(
            mixing, back_in[k].reshape(columns, width), preferred_element_type=jnp.float32
        )
        m = m[:2 * row_count] + m[2 * row_count:]
        out[:, k * span:k * span + width] = m[:row_count].astype(jnp.bfloat16)
        out[:, k * span + width:(k + 1) * span] = m[row_count:].astype(jnp.bfloat16)

    for t in range(chunks + 1):
        if t < chunks:
            down(t)
        if t >= 1:
            core_sum(t - 1)
    for t in range(chunks + 1):
        if t < chunks:
            side_sum(t)
        if t >= 1:
            mix(t - 1)

    for k in range(chunks):
        z_all(k).wait_send()
        y_copy(k).wait_send()
        c_copy(k).wait_send()
        cb_copy(k).wait_send()
        yb_copy(k).wait_send()
        zb_all(k).wait_send()


def local(tokens, expert_ids, keep_mask, tile_slot, route_weight, gate_weight, up_weight, down_weight):
    experts = lax.axis_size("loop") // SLICES
    row_count, model_width = tokens.shape
    units = gate_weight.shape[2]
    chunks = CHUNKS
    width = model_width // (2 * chunks)
    block = 2 * SEND
    rows = SLICES * experts * SEND
    bf16, f32 = jnp.bfloat16, jnp.float32
    vmem = pl.BlockSpec(memory_space=pltpu.VMEM)
    hbm = pl.BlockSpec(memory_space=pl.ANY)
    dma = pltpu.SemaphoreType.DMA
    return pl.pallas_call(
        functools.partial(kernel, experts),
        out_shape=jax.ShapeDtypeStruct((row_count, model_width), bf16),
        in_specs=[vmem, vmem, vmem, vmem, hbm, hbm, hbm],
        out_specs=vmem,
        scratch_shapes=[
            pltpu.VMEM((chunks, experts, block, width), bf16),
            pltpu.VMEM((chunks, SLICES, experts, block, width), bf16),
            pltpu.VMEM((model_width, units), bf16),
            pltpu.VMEM((model_width, units), bf16),
            pltpu.VMEM((units, model_width), bf16),
            pltpu.VMEM((rows, units), f32),
            pltpu.VMEM((rows, units), f32),
            pltpu.VMEM((chunks, 2, experts, block, width), f32),
            pltpu.VMEM((chunks, 2, experts, block, width), bf16),
            pltpu.VMEM((chunks, 2, experts, block, width), bf16),
            pltpu.VMEM((chunks, experts, block, width), bf16),
            pltpu.VMEM((chunks, experts, block, width), bf16),
            pltpu.VMEM((chunks, experts, block, width), bf16),
            pltpu.VMEM((chunks, experts, block, width), bf16),
            dma((3, chunks)),
        ] + [dma((chunks,)) for _ in range(12)],
        compiler_params=pltpu.CompilerParams(
            collective_id=0, has_side_effects=True, vmem_limit_bytes=56 * 1024 * 1024
        ),
        cost_estimate=pl.CostEstimate(
            flops=6 * rows * model_width * units,
            bytes_accessed=6 * model_width * units,
            transcendentals=rows * units,
        ),
    )(tokens, expert_ids, keep_mask, route_weight, gate_weight, up_weight, down_weight)


def solution(mesh):
    shared = P(("groups", "loop"), None)
    held = P("loop", None, None)
    return jax.shard_map(
        local,
        mesh=mesh,
        in_specs=(shared,) * 5 + (held,) * 3,
        out_specs=shared,
        check_vma=False,
    )
```

```python
import functools

import jax
import jax.numpy as jnp
from jax import lax
from jax.experimental import pallas as pl
from jax.experimental.pallas import tpu as pltpu
from jax.sharding import PartitionSpec as P

SLICES = 4
SEND = 8
CHUNKS = 2
AHEAD = 2
MESH = pl.DeviceIdType.MESH


def kernel(
    experts,
    tokens, ids, keep, route, gate_hbm, up_hbm, down_hbm,
    out,
    outgoing, tile, gate_w, up_w, down_w, gate_acc, up_acc, own_part,
    core_out, core_in, side_out, side_in, back_out, back_in,
    weight_sem, z_send, z_recv, y_send, y_recv, c_send, c_recv,
    cb_send, cb_recv, yb_send, yb_recv, zb_send, zb_recv,
):
    place = lax.axis_index("loop")
    mine = lax.div(place, SLICES)
    part = lax.rem(place, SLICES)
    side = mine * SLICES + lax.rem(part + 2, SLICES)
    core = mine * SLICES + part + 1 - 2 * lax.rem(part, 2)

    def along(step):
        return lax.rem(mine + step + experts, experts) * SLICES + part

    chunks = outgoing.shape[0]
    width = outgoing.shape[-1]
    span = 2 * width
    block = 2 * SEND
    columns = experts * block
    rows = SLICES * experts * SEND
    others = pl.ds(1, experts - 1)

    barrier = pltpu.get_barrier_semaphore()
    for step in range(1, experts):
        pl.semaphore_signal(barrier, inc=1, device_id={"loop": along(step)}, device_id_type=MESH)
    pl.semaphore_signal(barrier, inc=1, device_id={"loop": side}, device_id_type=MESH)
    pl.semaphore_signal(barrier, inc=1, device_id={"loop": core}, device_id_type=MESH)

    loads = []
    for k in range(chunks):
        at = pl.ds(k * span, span)
        loads.append((
            pltpu.make_async_copy(gate_hbm.at[0, at], gate_w.at[at], weight_sem.at[0, k]),
            pltpu.make_async_copy(up_hbm.at[0, at], up_w.at[at], weight_sem.at[1, k]),
        ))
        for load in loads[-1]:
            load.start()
    down_load = pltpu.make_async_copy(down_hbm.at[0], down_w, weight_sem.at[2, 0])
    down_load.start()

    row_count = tokens.shape[0]
    row = lax.broadcasted_iota(jnp.int32, (columns, row_count), 0)
    expert_of = lax.rem(mine - lax.div(row, block) + experts, experts)
    position_of = lax.rem(row, SEND)
    lower = lax.rem(row, block) < SEND
    chosen = jnp.where(keep[...] == 1, ids[...], -1)
    weights = route[...]
    live = jnp.zeros((columns, row_count), jnp.float32)
    scale = jnp.zeros((columns, row_count), jnp.float32)
    for k in range(ids.shape[0]):
        match = chosen[k:k + 1] == expert_of
        live = jnp.where(match, 1.0, live)
        scale = jnp.where(match, weights[k:k + 1], scale)
    earlier = (
        lax.broadcasted_iota(jnp.int32, (row_count, row_count), 0)
        < lax.broadcasted_iota(jnp.int32, (row_count, row_count), 1)
    ).astype(jnp.bfloat16)
    before = jnp.dot(live.astype(jnp.bfloat16), earlier, preferred_element_type=jnp.float32)
    select = jnp.where(before == position_of.astype(jnp.float32), live, 0.0)
    select_low = jnp.where(lower, select, 0.0)
    select_high = jnp.where(lower, 0.0, select)
    pick = jnp.concatenate([select_low, select_high], axis=1).astype(jnp.bfloat16)

    def z_copy(k, d):
        return pltpu.make_async_remote_copy(
            src_ref=outgoing.at[k, d], dst_ref=tile.at[k, 0, d],
            send_sem=z_send.at[k], recv_sem=z_recv.at[k],
            device_id={"loop": along(-d)}, device_id_type=MESH,
        )

    def z_start(k):
        for d in range(1, experts):
            z_copy(k, d).start()

    def z_all(k):
        return pltpu.make_async_remote_copy(
            src_ref=outgoing.at[k, others],
            dst_ref=tile.at[k, 0, others],
            send_sem=z_send.at[k], recv_sem=z_recv.at[k],
            device_id={"loop": along(1)}, device_id_type=MESH,
        )

    def y_copy(k):
        return pltpu.make_async_remote_copy(
            src_ref=tile.at[k, 0, others], dst_ref=tile.at[k, 1, others],
            send_sem=y_send.at[k], recv_sem=y_recv.at[k],
            device_id={"loop": side}, device_id_type=MESH,
        )

    def y_own():
        return pltpu.make_async_remote_copy(
            src_ref=tile.at[:, 0, 0], dst_ref=tile.at[:, 1, 0],
            send_sem=y_send.at[chunks], recv_sem=y_recv.at[chunks],
            device_id={"loop": side}, device_id_type=MESH,
        )

    def c_copy(k):
        return pltpu.make_async_remote_copy(
            src_ref=tile.at[k, pl.ds(0, 2)], dst_ref=tile.at[k, pl.ds(2, 2)],
            send_sem=c_send.at[k], recv_sem=c_recv.at[k],
            device_id={"loop": core}, device_id_type=MESH,
        )

    for k in range(chunks):
        low = tokens[:, k * span:k * span + width]
        high = tokens[:, k * span + width:(k + 1) * span]
        picked = jnp.dot(
            pick, jnp.concatenate([low, high], axis=0), preferred_element_type=jnp.float32
        ).astype(jnp.bfloat16).reshape(experts, block, width)
        outgoing[k] = picked
        tile[k, 0, 0] = picked[0]
        if k == 0:
            pl.semaphore_wait(barrier, experts + 1)
        if k < AHEAD:
            z_start(k)
    y_own().start()

    def gate_up(k):
        arrived = tile[k].astype(jnp.float32).reshape(SLICES * experts, block, width)
        x = jnp.concatenate(
            [arrived[:, :SEND].reshape(rows, width), arrived[:, SEND:].reshape(rows, width)], axis=1
        ).astype(jnp.bfloat16)
        for load in loads[k]:
            load.wait()
        at = pl.ds(k * span, span)
        gate = jnp.dot(x, gate_w[at], preferred_element_type=jnp.float32)
        up = jnp.dot(x, up_w[at], preferred_element_type=jnp.float32)
        if k == 0:
            gate_acc[...] = gate
            up_acc[...] = up
        else:
            gate_acc[...] += gate
            up_acc[...] += up

    for t in range(chunks + 2):
        if t < chunks:
            z_all(t).wait_recv()
            y_copy(t).start()
            if t + AHEAD < chunks:
                z_start(t + AHEAD)
        if t == 1:
            y_own().wait_recv()
        if 0 <= t - 1 < chunks:
            y_copy(t - 1).wait_recv()
            c_copy(t - 1).start()
        if 0 <= t - 2 < chunks:
            c_copy(t - 2).wait_recv()
            gate_up(t - 2)

    gate = gate_acc[...]
    hidden = (gate / (1.0 + jnp.exp(-gate)) * up_acc[...]).astype(jnp.bfloat16)
    down_load.wait()

    def cb_copy(k):
        return pltpu.make_async_remote_copy(
            src_ref=core_out.at[k], dst_ref=core_in.at[k],
            send_sem=cb_send.at[k], recv_sem=cb_recv.at[k],
            device_id={"loop": core}, device_id_type=MESH,
        )

    def yb_copy(k):
        return pltpu.make_async_remote_copy(
            src_ref=side_out.at[k, others], dst_ref=side_in.at[k, others],
            send_sem=yb_send.at[k], recv_sem=yb_recv.at[k],
            device_id={"loop": side}, device_id_type=MESH,
        )

    def yb_own():
        return pltpu.make_async_remote_copy(
            src_ref=side_out.at[:, 0], dst_ref=side_in.at[:, 0],
            send_sem=yb_send.at[chunks], recv_sem=yb_recv.at[chunks],
            device_id={"loop": side}, device_id_type=MESH,
        )

    def zb_copy(k, d):
        return pltpu.make_async_remote_copy(
            src_ref=back_out.at[k, d], dst_ref=back_in.at[k, d],
            send_sem=zb_send.at[k], recv_sem=zb_recv.at[k],
            device_id={"loop": along(d)}, device_id_type=MESH,
        )

    def zb_all(k):
        return pltpu.make_async_remote_copy(
            src_ref=back_out.at[k, others],
            dst_ref=back_in.at[k, others],
            send_sem=zb_send.at[k], recv_sem=zb_recv.at[k],
            device_id={"loop": along(1)}, device_id_type=MESH,
        )

    scaled = jnp.concatenate([select_low * scale, select_high * scale], axis=1).T
    coarse = scaled.astype(jnp.bfloat16)
    fine = (scaled - coarse.astype(jnp.float32)).astype(jnp.bfloat16)
    mixing = jnp.concatenate([coarse, fine], axis=0)

    def down(k):
        y = jnp.dot(hidden, down_w[:, k * span:(k + 1) * span], preferred_element_type=jnp.float32)
        y = jnp.concatenate(
            [
                y[:, :width].reshape(SLICES * experts, SEND, width),
                y[:, width:].reshape(SLICES * experts, SEND, width),
            ],
            axis=1,
        ).reshape(SLICES, experts, block, width)
        core_out[k] = y[2:].astype(jnp.bfloat16)
        cb_copy(k).start()
        own_part[k] = y[:2]

    def core_sum(k):
        cb_copy(k).wait_recv()
        side_out[k] = (own_part[k, 1] + core_in[k, 1].astype(jnp.float32)).astype(jnp.bfloat16)
        if k < AHEAD:
            yb_copy(k).start()
        own_part[k, 0] = own_part[k, 0] + core_in[k, 0].astype(jnp.float32)

    def side_sum(k):
        yb_copy(k).wait_recv()
        if k + AHEAD < chunks:
            yb_copy(k + AHEAD).start()
        if k == max(0, chunks - 1 - AHEAD):
            yb_own().start()
        total = own_part[k, 0, 1:] + side_in[k, 1:].astype(jnp.float32)
        back_out[k, 1:] = total.astype(jnp.bfloat16)
        for d in range(1, experts):
            zb_copy(k, d).start()

    def mix(k):
        back_in[k, 0] = (own_part[k, 0, 0] + side_in[k, 0].astype(jnp.float32)).astype(jnp.bfloat16)
        zb_all(k).wait_recv()
        m = jnp.dot(
            mixing, back_in[k].reshape(columns, width), preferred_element_type=jnp.float32
        )
        m = m[:2 * row_count] + m[2 * row_count:]
        out[:, k * span:k * span + width] = m[:row_count].astype(jnp.bfloat16)
        out[:, k * span + width:(k + 1) * span] = m[row_count:].astype(jnp.bfloat16)

    for t in range(chunks + 1):
        if t < chunks:
            down(t)
        if t >= 1:
            core_sum(t - 1)
    for k in range(chunks):
        side_sum(k)
    yb_own().wait_recv()
    for k in range(chunks):
        mix(k)

    y_own().wait_send()
    yb_own().wait_send()
    for k in range(chunks):
        z_all(k).wait_send()
        y_copy(k).wait_send()
        c_copy(k).wait_send()
        cb_copy(k).wait_send()
        yb_copy(k).wait_send()
        zb_all(k).wait_send()


def local(tokens, expert_ids, keep_mask, tile_slot, route_weight, gate_weight, up_weight, down_weight):
    experts = lax.axis_size("loop") // SLICES
    row_count, model_width = tokens.shape
    units = gate_weight.shape[2]
    chunks = CHUNKS
    width = model_width // (2 * chunks)
    block = 2 * SEND
    rows = SLICES * experts * SEND
    bf16, f32 = jnp.bfloat16, jnp.float32
    vmem = pl.BlockSpec(memory_space=pltpu.VMEM)
    hbm = pl.BlockSpec(memory_space=pl.ANY)
    dma = pltpu.SemaphoreType.DMA
    return pl.pallas_call(
        functools.partial(kernel, experts),
        out_shape=jax.ShapeDtypeStruct((row_count, model_width), bf16),
        in_specs=[vmem, vmem, vmem, vmem, hbm, hbm, hbm],
        out_specs=vmem,
        scratch_shapes=[
            pltpu.VMEM((chunks, experts, block, width), bf16),
            pltpu.VMEM((chunks, SLICES, experts, block, width), bf16),
            pltpu.VMEM((model_width, units), bf16),
            pltpu.VMEM((model_width, units), bf16),
            pltpu.VMEM((units, model_width), bf16),
            pltpu.VMEM((rows, units), f32),
            pltpu.VMEM((rows, units), f32),
            pltpu.VMEM((chunks, 2, experts, block, width), f32),
            pltpu.VMEM((chunks, 2, experts, block, width), bf16),
            pltpu.VMEM((chunks, 2, experts, block, width), bf16),
            pltpu.VMEM((chunks, experts, block, width), bf16),
            pltpu.VMEM((chunks, experts, block, width), bf16),
            pltpu.VMEM((chunks, experts, block, width), bf16),
            pltpu.VMEM((chunks, experts, block, width), bf16),
            dma((3, chunks)),
        ] + [dma((chunks + 1,)) for _ in range(12)],
        compiler_params=pltpu.CompilerParams(
            collective_id=0, has_side_effects=True, vmem_limit_bytes=56 * 1024 * 1024
        ),
        cost_estimate=pl.CostEstimate(
            flops=6 * rows * model_width * units,
            bytes_accessed=6 * model_width * units,
            transcendentals=rows * units,
        ),
    )(tokens, expert_ids.T, keep_mask.T, route_weight.T, gate_weight, up_weight, down_weight)


def solution(mesh):
    shared = P(("groups", "loop"), None)
    held = P("loop", None, None)
    return jax.shard_map(
        local,
        mesh=mesh,
        in_specs=(shared,) * 5 + (held,) * 3,
        out_specs=shared,
        check_vma=False,
    )
```

```python
import functools

import jax
import jax.numpy as jnp
from jax import lax
from jax.experimental import pallas as pl
from jax.experimental.pallas import tpu as pltpu
from jax.sharding import PartitionSpec as P

SLICES = 4
SEND = 8
CHUNKS = 4
AHEAD = 2
MESH = pl.DeviceIdType.MESH


def kernel(
    experts,
    tokens, ids, keep, route, gate_hbm, up_hbm, down_hbm,
    out,
    outgoing, tile, gate_w, up_w, down_w, gate_acc, up_acc, own_part,
    side_out, side_in, back_out, back_in,
    weight_sem, push_send, push_recv, z_send, z_recv, y_send, y_recv,
    yb_send, yb_recv, zb_send, zb_recv,
):
    place = lax.axis_index("loop")
    mine = lax.div(place, SLICES)
    part = lax.rem(place, SLICES)
    side = mine * SLICES + lax.rem(part + 2, SLICES)
    core = mine * SLICES + part + 1 - 2 * lax.rem(part, 2)

    def along(step):
        return lax.rem(mine + step + experts, experts) * SLICES + part

    chunks = outgoing.shape[0]
    width = outgoing.shape[-1]
    span = 2 * width
    block = 2 * SEND
    columns = experts * block
    rows = 2 * experts * SEND
    others = pl.ds(1, experts - 1)

    barrier = pltpu.get_barrier_semaphore()
    for step in range(1, experts):
        pl.semaphore_signal(barrier, inc=1, device_id={"loop": along(step)}, device_id_type=MESH)
    pl.semaphore_signal(barrier, inc=1, device_id={"loop": side}, device_id_type=MESH)
    pl.semaphore_signal(barrier, inc=1, device_id={"loop": core}, device_id_type=MESH)

    loads = []
    for k in range(chunks):
        at = pl.ds(k * span, span)
        loads.append((
            pltpu.make_async_copy(gate_hbm.at[0, at], gate_w.at[0, at], weight_sem.at[0, k]),
            pltpu.make_async_copy(up_hbm.at[0, at], up_w.at[0, at], weight_sem.at[1, k]),
        ))
        for load in loads[-1]:
            load.start()
    down_load = pltpu.make_async_copy(down_hbm.at[0], down_w.at[0], weight_sem.at[2, 0])
    down_load.start()

    row_count = tokens.shape[0]
    row = lax.broadcasted_iota(jnp.int32, (columns, row_count), 0)
    expert_of = lax.rem(mine - lax.div(row, block) + experts, experts)
    position_of = lax.rem(row, SEND)
    lower = lax.rem(row, block) < SEND
    chosen = jnp.where(keep[...] == 1, ids[...], -1)
    weights = route[...]
    live = jnp.zeros((columns, row_count), jnp.float32)
    scale = jnp.zeros((columns, row_count), jnp.float32)
    for k in range(ids.shape[0]):
        match = chosen[k:k + 1] == expert_of
        live = jnp.where(match, 1.0, live)
        scale = jnp.where(match, weights[k:k + 1], scale)
    earlier = (
        lax.broadcasted_iota(jnp.int32, (row_count, row_count), 0)
        < lax.broadcasted_iota(jnp.int32, (row_count, row_count), 1)
    ).astype(jnp.bfloat16)
    before = jnp.dot(live.astype(jnp.bfloat16), earlier, preferred_element_type=jnp.float32)
    select = jnp.where(before == position_of.astype(jnp.float32), live, 0.0)
    select_low = jnp.where(lower, select, 0.0)
    select_high = jnp.where(lower, 0.0, select)
    pick = jnp.concatenate([select_low, select_high], axis=1).astype(jnp.bfloat16)

    def z_copy(k, d):
        return pltpu.make_async_remote_copy(
            src_ref=outgoing.at[k, d], dst_ref=tile.at[k, 0, d],
            send_sem=z_send.at[k], recv_sem=z_recv.at[k],
            device_id={"loop": along(-d)}, device_id_type=MESH,
        )

    def z_start(k):
        for d in range(1, experts):
            z_copy(k, d).start()

    def z_all(k):
        return pltpu.make_async_remote_copy(
            src_ref=outgoing.at[k, others],
            dst_ref=tile.at[k, 0, others],
            send_sem=z_send.at[k], recv_sem=z_recv.at[k],
            device_id={"loop": along(1)}, device_id_type=MESH,
        )

    def y_copy(k):
        return pltpu.make_async_remote_copy(
            src_ref=tile.at[k, 0, others], dst_ref=tile.at[k, 1, others],
            send_sem=y_send.at[k], recv_sem=y_recv.at[k],
            device_id={"loop": side}, device_id_type=MESH,
        )

    def y_own():
        return pltpu.make_async_remote_copy(
            src_ref=tile.at[:, 0, 0], dst_ref=tile.at[:, 1, 0],
            send_sem=y_send.at[chunks], recv_sem=y_recv.at[chunks],
            device_id={"loop": side}, device_id_type=MESH,
        )

    def push(which, k):
        at = pl.ds(k * span, span)
        source, target = (
            (gate_hbm.at[0, at], gate_w.at[1, at]),
            (up_hbm.at[0, at], up_w.at[1, at]),
            (down_hbm.at[0, :, at], down_w.at[1, :, at]),
        )[which]
        return pltpu.make_async_remote_copy(
            src_ref=source, dst_ref=target,
            send_sem=push_send.at[which, k], recv_sem=push_recv.at[which, k],
            device_id={"loop": core}, device_id_type=MESH,
        )

    for k in range(chunks):
        low = tokens[:, k * span:k * span + width]
        high = tokens[:, k * span + width:(k + 1) * span]
        picked = jnp.dot(
            pick, jnp.concatenate([low, high], axis=0), preferred_element_type=jnp.float32
        ).astype(jnp.bfloat16).reshape(experts, block, width)
        outgoing[k] = picked
        tile[k, 0, 0] = picked[0]
        if k == 0:
            pl.semaphore_wait(barrier, experts + 1)
        if k < AHEAD:
            z_start(k)
        if k == 0:
            for i in range(chunks):
                push(0, i).start()
                push(1, i).start()
            for i in range(chunks):
                push(2, i).start()
    y_own().start()

    scaled = jnp.concatenate([select_low * scale, select_high * scale], axis=1).T
    coarse = scaled.astype(jnp.bfloat16)
    fine = (scaled - coarse.astype(jnp.float32)).astype(jnp.bfloat16)
    mixing = jnp.concatenate([coarse, fine], axis=0)

    def gate_up(k):
        arrived = tile[k].astype(jnp.float32).reshape(2 * experts, block, width)
        x = jnp.concatenate(
            [arrived[:, :SEND].reshape(rows, width), arrived[:, SEND:].reshape(rows, width)], axis=1
        ).astype(jnp.bfloat16)
        at = pl.ds(k * span, span)
        for j in range(2):
            if j == 0:
                for load in loads[k]:
                    load.wait()
            else:
                push(0, k).wait_recv()
                push(1, k).wait_recv()
            gate = jnp.dot(x, gate_w[j, at], preferred_element_type=jnp.float32)
            up = jnp.dot(x, up_w[j, at], preferred_element_type=jnp.float32)
            if k == 0:
                gate_acc[j] = gate
                up_acc[j] = up
            else:
                gate_acc[j] += gate
                up_acc[j] += up

    for t in range(chunks + 1):
        if t < chunks:
            z_all(t).wait_recv()
            y_copy(t).start()
            if t + AHEAD < chunks:
                z_start(t + AHEAD)
        if t == 1:
            y_own().wait_recv()
        if t >= 1:
            y_copy(t - 1).wait_recv()
            gate_up(t - 1)

    gate = gate_acc[...]
    hidden = (gate / (1.0 + jnp.exp(-gate)) * up_acc[...]).astype(jnp.bfloat16)
    down_load.wait()

    def yb_copy(k):
        return pltpu.make_async_remote_copy(
            src_ref=side_out.at[k, others], dst_ref=side_in.at[k, others],
            send_sem=yb_send.at[k], recv_sem=yb_recv.at[k],
            device_id={"loop": side}, device_id_type=MESH,
        )

    def yb_own():
        return pltpu.make_async_remote_copy(
            src_ref=side_out.at[:, 0], dst_ref=side_in.at[:, 0],
            send_sem=yb_send.at[chunks], recv_sem=yb_recv.at[chunks],
            device_id={"loop": side}, device_id_type=MESH,
        )

    def zb_copy(k, d):
        return pltpu.make_async_remote_copy(
            src_ref=back_out.at[k, d], dst_ref=back_in.at[k, d],
            send_sem=zb_send.at[k], recv_sem=zb_recv.at[k],
            device_id={"loop": along(d)}, device_id_type=MESH,
        )

    def zb_all(k):
        return pltpu.make_async_remote_copy(
            src_ref=back_out.at[k, others],
            dst_ref=back_in.at[k, others],
            send_sem=zb_send.at[k], recv_sem=zb_recv.at[k],
            device_id={"loop": along(1)}, device_id_type=MESH,
        )

    def down(k):
        push(2, k).wait_recv()
        at = pl.ds(k * span, span)
        y = jnp.dot(hidden[0], down_w[0, :, at], preferred_element_type=jnp.float32)
        y += jnp.dot(hidden[1], down_w[1, :, at], preferred_element_type=jnp.float32)
        y = jnp.concatenate(
            [
                y[:, :width].reshape(2 * experts, SEND, width),
                y[:, width:].reshape(2 * experts, SEND, width),
            ],
            axis=1,
        ).reshape(2, experts, block, width)
        side_out[k] = y[1].astype(jnp.bfloat16)
        if k < AHEAD:
            yb_copy(k).start()
        own_part[k] = y[0]

    def side_sum(k):
        yb_copy(k).wait_recv()
        if k + AHEAD < chunks:
            yb_copy(k + AHEAD).start()
        if k == max(0, chunks - 1 - AHEAD):
            yb_own().start()
        total = own_part[k, 1:] + side_in[k, 1:].astype(jnp.float32)
        back_out[k, 1:] = total.astype(jnp.bfloat16)
        for d in range(1, experts):
            zb_copy(k, d).start()

    def mix(k):
        back_in[k, 0] = (own_part[k, 0] + side_in[k, 0].astype(jnp.float32)).astype(jnp.bfloat16)
        zb_all(k).wait_recv()
        m = jnp.dot(
            mixing, back_in[k].reshape(columns, width), preferred_element_type=jnp.float32
        )
        m = m[:2 * row_count] + m[2 * row_count:]
        out[:, k * span:k * span + width] = m[:row_count].astype(jnp.bfloat16)
        out[:, k * span + width:(k + 1) * span] = m[row_count:].astype(jnp.bfloat16)

    for k in range(chunks):
        down(k)
    for k in range(chunks):
        side_sum(k)
    yb_own().wait_recv()
    for k in range(chunks):
        mix(k)

    y_own().wait_send()
    yb_own().wait_send()
    for k in range(chunks):
        z_all(k).wait_send()
        y_copy(k).wait_send()
        for i in range(3):
            push(i, k).wait_send()
        yb_copy(k).wait_send()
        zb_all(k).wait_send()


def local(tokens, expert_ids, keep_mask, tile_slot, route_weight, gate_weight, up_weight, down_weight):
    experts = lax.axis_size("loop") // SLICES
    row_count, model_width = tokens.shape
    units = gate_weight.shape[2]
    chunks = CHUNKS
    width = model_width // (2 * chunks)
    block = 2 * SEND
    rows = 2 * experts * SEND
    bf16, f32 = jnp.bfloat16, jnp.float32
    vmem = pl.BlockSpec(memory_space=pltpu.VMEM)
    hbm = pl.BlockSpec(memory_space=pl.ANY)
    dma = pltpu.SemaphoreType.DMA
    return pl.pallas_call(
        functools.partial(kernel, experts),
        out_shape=jax.ShapeDtypeStruct((row_count, model_width), bf16),
        in_specs=[vmem, vmem, vmem, vmem, hbm, hbm, hbm],
        out_specs=vmem,
        scratch_shapes=[
            pltpu.VMEM((chunks, experts, block, width), bf16),
            pltpu.VMEM((chunks, 2, experts, block, width), bf16),
            pltpu.VMEM((2, model_width, units), bf16),
            pltpu.VMEM((2, model_width, units), bf16),
            pltpu.VMEM((2, units, model_width), bf16),
            pltpu.VMEM((2, rows, units), f32),
            pltpu.VMEM((2, rows, units), f32),
            pltpu.VMEM((chunks, experts, block, width), f32),
            pltpu.VMEM((chunks, experts, block, width), bf16),
            pltpu.VMEM((chunks, experts, block, width), bf16),
            pltpu.VMEM((chunks, experts, block, width), bf16),
            pltpu.VMEM((chunks, experts, block, width), bf16),
            dma((3, chunks)),
            dma((3, chunks)),
            dma((3, chunks)),
        ] + [dma((chunks + 1,)) for _ in range(8)],
        compiler_params=pltpu.CompilerParams(
            collective_id=0, has_side_effects=True, vmem_limit_bytes=56 * 1024 * 1024
        ),
        cost_estimate=pl.CostEstimate(
            flops=12 * rows * model_width * units,
            bytes_accessed=6 * model_width * units,
            transcendentals=2 * rows * units,
        ),
    )(tokens, expert_ids.T, keep_mask.T, route_weight.T, gate_weight, up_weight, down_weight)


def solution(mesh):
    shared = P(("groups", "loop"), None)
    held = P("loop", None, None)
    return jax.shard_map(
        local,
        mesh=mesh,
        in_specs=(shared,) * 5 + (held,) * 3,
        out_specs=shared,
        check_vma=False,
    )
```

```python
import functools

import jax
import jax.numpy as jnp
from jax import lax
from jax.experimental import pallas as pl
from jax.experimental.pallas import tpu as pltpu
from jax.sharding import PartitionSpec as P

SLICES = 4
SEND = 8
CHUNKS = 4
AHEAD = 2
AHEAD_BACK = 4
MESH = pl.DeviceIdType.MESH


def kernel(
    experts,
    tokens, ids, keep, route, gate_hbm, up_hbm, down_hbm,
    out_hbm,
    outgoing, tile, gate_w, up_w, down_w, gate_acc, up_acc, own_part,
    side_out, side_in, back_out, back_in, out, out_sem,
    weight_sem, push_send, push_recv, z_send, z_recv, y_send, y_recv,
    yb_send, yb_recv, zb_send, zb_recv,
):
    place = lax.axis_index("loop")
    mine = lax.div(place, SLICES)
    part = lax.rem(place, SLICES)
    side = mine * SLICES + lax.rem(part + 2, SLICES)
    core = mine * SLICES + part + 1 - 2 * lax.rem(part, 2)

    def along(step):
        return lax.rem(mine + step + experts, experts) * SLICES + part

    chunks = outgoing.shape[0]
    width = outgoing.shape[-1]
    span = 2 * width
    block = 2 * SEND
    columns = experts * block
    rows = 2 * experts * SEND
    others = pl.ds(1, experts - 1)

    barrier = pltpu.get_barrier_semaphore()
    for step in range(1, experts):
        pl.semaphore_signal(barrier, inc=1, device_id={"loop": along(step)}, device_id_type=MESH)
    pl.semaphore_signal(barrier, inc=1, device_id={"loop": side}, device_id_type=MESH)
    pl.semaphore_signal(barrier, inc=1, device_id={"loop": core}, device_id_type=MESH)

    loads = []
    for k in range(chunks):
        at = pl.ds(k * span, span)
        loads.append((
            pltpu.make_async_copy(gate_hbm.at[0, at], gate_w.at[0, at], weight_sem.at[0, k]),
            pltpu.make_async_copy(up_hbm.at[0, at], up_w.at[0, at], weight_sem.at[1, k]),
        ))
        for load in loads[-1]:
            load.start()
    down_load = pltpu.make_async_copy(down_hbm.at[0], down_w.at[0], weight_sem.at[2, 0])
    down_load.start()

    row_count = tokens.shape[0]
    row = lax.broadcasted_iota(jnp.int32, (columns, row_count), 0)
    expert_of = lax.rem(mine - lax.div(row, block) + experts, experts)
    position_of = lax.rem(row, SEND)
    lower = lax.rem(row, block) < SEND
    chosen = jnp.where(keep[...] == 1, ids[...], -1)
    weights = route[...]
    live = jnp.zeros((columns, row_count), jnp.float32)
    scale = jnp.zeros((columns, row_count), jnp.float32)
    for k in range(ids.shape[0]):
        match = chosen[k:k + 1] == expert_of
        live = jnp.where(match, 1.0, live)
        scale = jnp.where(match, weights[k:k + 1], scale)
    earlier = (
        lax.broadcasted_iota(jnp.int32, (row_count, row_count), 0)
        < lax.broadcasted_iota(jnp.int32, (row_count, row_count), 1)
    ).astype(jnp.bfloat16)
    before = jnp.dot(live.astype(jnp.bfloat16), earlier, preferred_element_type=jnp.float32)
    select = jnp.where(before == position_of.astype(jnp.float32), live, 0.0)
    select_low = jnp.where(lower, select, 0.0)
    select_high = jnp.where(lower, 0.0, select)
    pick = jnp.concatenate([select_low, select_high], axis=1).astype(jnp.bfloat16)

    def z_copy(k, d):
        return pltpu.make_async_remote_copy(
            src_ref=outgoing.at[k, d], dst_ref=tile.at[k, 0, d],
            send_sem=z_send.at[k], recv_sem=z_recv.at[k],
            device_id={"loop": along(-d)}, device_id_type=MESH,
        )

    def z_start(k):
        for d in range(1, experts):
            z_copy(k, d).start()

    def z_all(k):
        return pltpu.make_async_remote_copy(
            src_ref=outgoing.at[k, others],
            dst_ref=tile.at[k, 0, others],
            send_sem=z_send.at[k], recv_sem=z_recv.at[k],
            device_id={"loop": along(1)}, device_id_type=MESH,
        )

    def y_copy(k):
        return pltpu.make_async_remote_copy(
            src_ref=tile.at[k, 0, others], dst_ref=tile.at[k, 1, others],
            send_sem=y_send.at[k], recv_sem=y_recv.at[k],
            device_id={"loop": side}, device_id_type=MESH,
        )

    def y_own():
        return pltpu.make_async_remote_copy(
            src_ref=tile.at[:, 0, 0], dst_ref=tile.at[:, 1, 0],
            send_sem=y_send.at[chunks], recv_sem=y_recv.at[chunks],
            device_id={"loop": side}, device_id_type=MESH,
        )

    def push(which, k):
        at = pl.ds(k * span, span)
        source, target = (
            (gate_hbm.at[0, at], gate_w.at[1, at]),
            (up_hbm.at[0, at], up_w.at[1, at]),
            (down_hbm.at[0, :, at], down_w.at[1, :, at]),
        )[which]
        return pltpu.make_async_remote_copy(
            src_ref=source, dst_ref=target,
            send_sem=push_send.at[which, k], recv_sem=push_recv.at[which, k],
            device_id={"loop": core}, device_id_type=MESH,
        )

    for k in range(chunks):
        low = tokens[:, k * span:k * span + width]
        high = tokens[:, k * span + width:(k + 1) * span]
        picked = jnp.dot(
            pick, jnp.concatenate([low, high], axis=0), preferred_element_type=jnp.float32
        ).astype(jnp.bfloat16).reshape(experts, block, width)
        outgoing[k] = picked
        tile[k, 0, 0] = picked[0]
        if k == 0:
            pl.semaphore_wait(barrier, experts + 1)
        if k < AHEAD:
            z_start(k)
        if k == 0:
            for i in range(chunks):
                push(0, i).start()
                push(1, i).start()
            for i in range(chunks):
                push(2, i).start()
    y_own().start()

    scaled = jnp.concatenate([select_low * scale, select_high * scale], axis=1).T
    coarse = scaled.astype(jnp.bfloat16)
    fine = (scaled - coarse.astype(jnp.float32)).astype(jnp.bfloat16)
    mixing = jnp.concatenate([coarse, fine], axis=0)

    def gate_up(k):
        arrived = tile[k].astype(jnp.float32).reshape(2 * experts, block, width)
        x = jnp.concatenate(
            [arrived[:, :SEND].reshape(rows, width), arrived[:, SEND:].reshape(rows, width)], axis=1
        ).astype(jnp.bfloat16)
        at = pl.ds(k * span, span)
        for j in range(2):
            if j == 0:
                for load in loads[k]:
                    load.wait()
            else:
                push(0, k).wait_recv()
                push(1, k).wait_recv()
            gate = jnp.dot(x, gate_w[j, at], preferred_element_type=jnp.float32)
            up = jnp.dot(x, up_w[j, at], preferred_element_type=jnp.float32)
            if k == 0:
                gate_acc[j] = gate
                up_acc[j] = up
            else:
                gate_acc[j] += gate
                up_acc[j] += up

    for t in range(chunks + 1):
        if t < chunks:
            z_all(t).wait_recv()
            y_copy(t).start()
            if t + AHEAD < chunks:
                z_start(t + AHEAD)
        if t == 1:
            y_own().wait_recv()
        if t >= 1:
            y_copy(t - 1).wait_recv()
            gate_up(t - 1)

    gate = gate_acc[...]
    hidden = (gate / (1.0 + jnp.exp(-gate)) * up_acc[...]).astype(jnp.bfloat16)
    down_load.wait()

    def yb_copy(k):
        return pltpu.make_async_remote_copy(
            src_ref=side_out.at[k, others], dst_ref=side_in.at[k, others],
            send_sem=yb_send.at[k], recv_sem=yb_recv.at[k],
            device_id={"loop": side}, device_id_type=MESH,
        )

    def yb_own():
        return pltpu.make_async_remote_copy(
            src_ref=side_out.at[:, 0], dst_ref=side_in.at[:, 0],
            send_sem=yb_send.at[chunks], recv_sem=yb_recv.at[chunks],
            device_id={"loop": side}, device_id_type=MESH,
        )

    def zb_copy(k, d):
        return pltpu.make_async_remote_copy(
            src_ref=back_out.at[k, d], dst_ref=back_in.at[k, d],
            send_sem=zb_send.at[k], recv_sem=zb_recv.at[k],
            device_id={"loop": along(d)}, device_id_type=MESH,
        )

    def zb_all(k):
        return pltpu.make_async_remote_copy(
            src_ref=back_out.at[k, others],
            dst_ref=back_in.at[k, others],
            send_sem=zb_send.at[k], recv_sem=zb_recv.at[k],
            device_id={"loop": along(1)}, device_id_type=MESH,
        )

    def down(k):
        push(2, k).wait_recv()
        at = pl.ds(k * span, span)
        y = jnp.dot(hidden[0], down_w[0, :, at], preferred_element_type=jnp.float32)
        y += jnp.dot(hidden[1], down_w[1, :, at], preferred_element_type=jnp.float32)
        y = jnp.concatenate(
            [
                y[:, :width].reshape(2 * experts, SEND, width),
                y[:, width:].reshape(2 * experts, SEND, width),
            ],
            axis=1,
        ).reshape(2, experts, block, width)
        side_out[k] = y[1].astype(jnp.bfloat16)
        if k < AHEAD_BACK:
            yb_copy(k).start()
        own_part[k] = y[0]

    def side_sum(k):
        yb_copy(k).wait_recv()
        if k + AHEAD_BACK < chunks:
            yb_copy(k + AHEAD_BACK).start()
        if k == max(0, chunks - 1 - AHEAD_BACK):
            yb_own().start()
        total = own_part[k, 1:] + side_in[k, 1:].astype(jnp.float32)
        back_out[k, 1:] = total.astype(jnp.bfloat16)
        for d in range(1, experts):
            zb_copy(k, d).start()

    def store(k):
        at = pl.ds(k * span, span)
        return pltpu.make_async_copy(out.at[:, at], out_hbm.at[:, at], out_sem.at[k])

    def mix(k):
        back_in[k, 0] = (own_part[k, 0] + side_in[k, 0].astype(jnp.float32)).astype(jnp.bfloat16)
        zb_all(k).wait_recv()
        m = jnp.dot(
            mixing, back_in[k].reshape(columns, width), preferred_element_type=jnp.float32
        )
        m = m[:2 * row_count] + m[2 * row_count:]
        out[:, k * span:k * span + width] = m[:row_count].astype(jnp.bfloat16)
        out[:, k * span + width:(k + 1) * span] = m[row_count:].astype(jnp.bfloat16)

    for k in range(chunks):
        down(k)
    for k in range(chunks):
        side_sum(k)
    yb_own().wait_recv()
    for k in range(chunks):
        mix(k)
        store(k).start()

    y_own().wait_send()
    yb_own().wait_send()
    for k in range(chunks):
        z_all(k).wait_send()
        y_copy(k).wait_send()
        for i in range(3):
            push(i, k).wait_send()
        store(k).wait()
        yb_copy(k).wait_send()
        zb_all(k).wait_send()


def local(tokens, expert_ids, keep_mask, tile_slot, route_weight, gate_weight, up_weight, down_weight):
    experts = lax.axis_size("loop") // SLICES
    row_count, model_width = tokens.shape
    units = gate_weight.shape[2]
    chunks = CHUNKS
    width = model_width // (2 * chunks)
    block = 2 * SEND
    rows = 2 * experts * SEND
    bf16, f32 = jnp.bfloat16, jnp.float32
    vmem = pl.BlockSpec(memory_space=pltpu.VMEM)
    hbm = pl.BlockSpec(memory_space=pl.ANY)
    dma = pltpu.SemaphoreType.DMA
    return pl.pallas_call(
        functools.partial(kernel, experts),
        out_shape=jax.ShapeDtypeStruct((row_count, model_width), bf16),
        in_specs=[vmem, vmem, vmem, vmem, hbm, hbm, hbm],
        out_specs=hbm,
        scratch_shapes=[
            pltpu.VMEM((chunks, experts, block, width), bf16),
            pltpu.VMEM((chunks, 2, experts, block, width), bf16),
            pltpu.VMEM((2, model_width, units), bf16),
            pltpu.VMEM((2, model_width, units), bf16),
            pltpu.VMEM((2, units, model_width), bf16),
            pltpu.VMEM((2, rows, units), f32),
            pltpu.VMEM((2, rows, units), f32),
            pltpu.VMEM((chunks, experts, block, width), f32),
            pltpu.VMEM((chunks, experts, block, width), bf16),
            pltpu.VMEM((chunks, experts, block, width), bf16),
            pltpu.VMEM((chunks, experts, block, width), bf16),
            pltpu.VMEM((chunks, experts, block, width), bf16),
            pltpu.VMEM((row_count, model_width), bf16),
            dma((chunks,)),
            dma((3, chunks)),
            dma((3, chunks)),
            dma((3, chunks)),
        ] + [dma((chunks + 1,)) for _ in range(8)],
        compiler_params=pltpu.CompilerParams(
            collective_id=0, has_side_effects=True, vmem_limit_bytes=56 * 1024 * 1024
        ),
        cost_estimate=pl.CostEstimate(
            flops=12 * rows * model_width * units,
            bytes_accessed=6 * model_width * units,
            transcendentals=2 * rows * units,
        ),
    )(tokens, expert_ids.T, keep_mask.T, route_weight.T, gate_weight, up_weight, down_weight)


def solution(mesh):
    shared = P(("groups", "loop"), None)
    held = P("loop", None, None)
    return jax.shard_map(
        local,
        mesh=mesh,
        in_specs=(shared,) * 5 + (held,) * 3,
        out_specs=shared,
        check_vma=False,
    )
```
